256 devices in a mesh: row: 8 (over z), col: 32 (over x, y, core).
Axes of the slice: x: 4, y: 4, z: 8, core: 2. Of those that a mesh axis runs over, the one named last changes fastest.
Arguments:
- activations: bfloat16 [131072, 8192], P(('row', 'col')), may hold values from -24 to 24
- kv_grads: bfloat16 [131072, 512], P(('row', 'col')), may hold values from -24 to 24
- row_state: float32 [512], P('row'), may hold values from 0.01 to 1
- col_state: float32 [2, 8192], P(None, 'col'), may hold values from 0.01 to 1
Outputs:
- direction: float32 [512, 8192], P('row', 'col')
- row_new: float32 [512], P('row')
- col_new: float32 [2, 8192], P(None, 'col')
The draws below stay inside these ranges and needn't reach their ends.
All inputs are finite; a program needn't handle non-finite values.
Results may differ from the reference program's by a relative error of at most 0.0003.
Values sent between devices are 32-bit elements; how exact they have to be, the bound alone decides.
No kernel may reach another device: no remote copies, remote signals or barrier semaphores. Data moves between devices by JAX's collectives and lax.ppermute only.
A program may use at most 256 MiB of HBM per device.

```python
import math
import jax
import jax.numpy as jnp
from jax import lax

D = 8192
HEAD_DIM = 256
TOK_DEV = 512
KV = 512
TOKENS = 131072
N_ROW = 8
N_COL = 32


def column_scales(key, width):
    return jnp.exp(jax.random.uniform(key, (width,), jnp.float32, math.log(0.3), math.log(3.0)))


def draw_activations(key, part):
    key = jax.random.fold_in(key, 11)
    key_scale, key_main = jax.random.split(key, 2)
    scales = column_scales(key_scale, D)
    values = jnp.clip(jax.random.normal(key_main, (TOKENS, D), jnp.float32), -4.0, 4.0) * scales[None, :]
    return values.astype(jnp.bfloat16)


def draw_kv_grads(key, part):
    key = jax.random.fold_in(key, 23)
    key_scale, key_main = jax.random.split(key, 2)
    scales = column_scales(key_scale, KV)
    values = jnp.clip(jax.random.normal(key_main, (TOKENS, KV), jnp.float32), -4.0, 4.0) * scales[None, :]
    return values.astype(jnp.bfloat16)


def draw_row_state(key, part):
    key = jax.random.fold_in(key, 37)
    position = jnp.arange(KV, dtype=jnp.float32) / (KV - 1)
    rising = jnp.exp(math.log(10.0) * position)
    base = jnp.exp(jax.random.uniform(key, (KV,), jnp.float32, math.log(0.01), math.log(0.1)))
    return base * rising


def level_of(key, shape, pieces, smallest, largest):
    gain = 1.0
    for dim, shards_of in pieces:
        draws = jax.random.uniform(jax.random.fold_in(jax.random.fold_in(key, 6), dim), (shards_of,), jnp.float32, smallest / len(pieces), largest / len(pieces))
        gain = gain * jnp.repeat(jnp.exp(draws), shape[dim] // shards_of).reshape((-1,) + (1,) * (len(shape) - 1 - dim))
    return gain


def setup_inputs(seed: int = 0) -> dict:
    key_list = jax.random.split(jax.random.key(seed), 5)
    return {
        "activations": draw_activations(jax.random.fold_in(key_list[4], 71), 0),
        "kv_grads": draw_kv_grads(jax.random.fold_in(key_list[4], 71), 0),
        "row_state": draw_row_state(jax.random.fold_in(key_list[4], 71), 0),
        "col_state": jnp.clip(jnp.exp(math.log(1.0) - 4.6051702 * jax.random.uniform(key_list[3], (2, D), jnp.float32) ** level_of(key_list[3], (2, D), ((1, 32),), -0.2, 0.2)), 0.01, 1.0),
    }


DECAY_RATE = 1.0 - 8.0 ** (-0.8)
EPSILON = 1e-30
CLIP_LIMIT = 1.0

def reference(activations, kv_grads, row_state, col_state):
    x_blocks = activations.reshape(N_ROW, TOK_DEV * N_COL, D)
    y_blocks = kv_grads.reshape(N_ROW, TOK_DEV * N_COL, KV)

    def accumulate(running, blocks):
        x_part, y_part = blocks
        return (running + lax.dot_general(y_part, x_part, (((0,), (0,)), ((), ())), preferred_element_type=jnp.float32), None)
    summed, _ = lax.scan(accumulate, jnp.zeros((KV, D), jnp.float32), (x_blocks, y_blocks))
    grad = summed * TOKENS ** (-0.5)
    squares = grad * grad + EPSILON
    row_new = DECAY_RATE * row_state + (1.0 - DECAY_RATE) * (lax.optimization_barrier(jnp.sum(squares, axis=1)) / D)
    col_new = DECAY_RATE * col_state + (1.0 - DECAY_RATE) * (lax.optimization_barrier(jnp.sum(squares.reshape(HEAD_DIM, 2, D), axis=0)) / HEAD_DIM)
    second_moment = row_new.reshape(HEAD_DIM, 2, 1) * col_new[None, :, :]
    raw_step = grad.reshape(HEAD_DIM, 2, D) / jnp.sqrt(second_moment)
    root_mean = jnp.sqrt(lax.optimization_barrier(jnp.sum(raw_step * raw_step, axis=(0, 2))) / (HEAD_DIM * D))
    limiter = jnp.maximum(1.0, root_mean / CLIP_LIMIT)
    direction = (raw_step / limiter[None, :, None]).reshape(KV, D)
    return (direction, row_new, col_new)
```

```python
import functools
import jax
import jax.numpy as jnp
import numpy as np
from jax import lax
from jax.experimental import pallas as pl
from jax.experimental.pallas import tpu as pltpu
from jax.sharding import PartitionSpec as P

D = 8192
HEAD_DIM = 256
DECAY_RATE = 1.0 - 8.0 ** (-0.8)
EPSILON = 1e-30
CLIP_LIMIT = 1.0

RING4 = ((1, 3), (3, 1))
RING8 = (1, 2, 6)
XYZ = "xyzxyzz"
YZX = "yzxyzxz"
ZXY = "zxyzxyz"
PARTS = (
    (0, 8, 0, 384, 0, XYZ),
    (8, 8, 0, 384, 1, XYZ),
    (16, 8, 0, 384, 0, YZX),
    (24, 8, 0, 384, 1, YZX),
    (0, 16, 384, 128, 0, ZXY),
    (16, 16, 384, 128, 1, ZXY),
)


def masks4(kind):
    first, second = RING4[kind]
    return [0, second, first, first ^ second]


def masks8():
    a, b, c = RING8
    return [i * a ^ j * b ^ k * c for i in (0, 1) for j in (0, 1) for k in (0, 1)]


def col_perm(axis, mask):
    if axis == "c":
        return [(i, i ^ 1) for i in range(32)]
    shift = 3 if axis == "x" else 1
    return [(i, i ^ (mask << shift)) for i in range(32)]


def row_perm(mask, kind):
    return [(i, (((i + kind) % 8) ^ mask) + 8 * kind - kind) for i in range(8)]


def row_pairs(mask, kind):
    return [(a, b % 8) for a, b in row_perm(mask, kind)]


def partial_kernel(count, places, x_ref, y_ref, *refs):
    got, out, acc = refs[:count], refs[count:-1], refs[-1]
    acc[...] = lax.dot_general(
        x_ref[...], y_ref[...], (((0,), (0,)), ((), ())), preferred_element_type=jnp.float32
    )
    for p, (row, rows, lane, lanes, kind, _) in enumerate(PARTS):
        for slot in range(8):
            start = pl.multiple_of(places[32 + kind * 8 + slot] * 32 + row, 8)
            value = acc[pl.ds(start, rows), lane : lane + lanes]
            if count:
                value = value + got[p][0, slot]
            out[p][0, slot] = value


def partial(places, x, y, got):
    shapes = [(16, 8, rows, lanes) for _, rows, _, lanes, _, _ in PARTS]
    blocks = []

    def spec(part):
        shape = shapes[part]
        kind = PARTS[part][4]
        return pl.BlockSpec((1,) + shape[1:], lambda s, places: (places[48 + 16 * kind + s], 0, 0, 0))

    specs = [spec(p) for p in range(len(PARTS))]
    return pl.pallas_call(
        functools.partial(partial_kernel, len(got)),
        grid_spec=pltpu.PrefetchScalarGridSpec(
            num_scalar_prefetch=1,
            grid=(16,),
            in_specs=[
                pl.BlockSpec((512, 256), lambda s, places: (0, places[s])),
                pl.BlockSpec((512, 512), lambda s, places: (0, 0)),
            ]
            + (specs if got else []),
            out_specs=specs,
            scratch_shapes=[pltpu.VMEM((256, 512), jnp.float32)],
        ),
        out_shape=[jax.ShapeDtypeStruct(s, jnp.float32) for s in shapes],
        compiler_params=pltpu.CompilerParams(vmem_limit_bytes=24 * 1024 * 1024),
        cost_estimate=pl.CostEstimate(
            flops=2 * 512 * 512 * 4096, bytes_accessed=13_000_000 + 8_400_000 * (len(got) > 0), transcendentals=0
        ),
    )(places, x, y, *got)


def reduce_parts(parts):
    values = []
    dims = []
    for part, (_, rows, _, lanes, _, _) in zip(parts, PARTS):
        values.append(part.reshape((2, 2, 2, 2, 2, 2, 2, rows, lanes)))
        dims.append([("x", 0), ("x", 1), ("y", 0), ("y", 1), ("z", 0), ("z", 1), ("z", 2)])
    done = [{"x": 0, "y": 0, "z": 0} for _ in PARTS]
    for step in range(7):
        sent = []
        for p, (_, _, _, _, kind, order) in enumerate(PARTS):
            axis = order[step]
            at = dims[p].index((axis, done[p][axis]))
            send = lax.index_in_dim(values[p], 1, at, keepdims=False)
            if axis == "z":
                got = lax.ppermute(send, "row", row_pairs(RING8[done[p][axis]], kind))
            else:
                got = lax.ppermute(send, "col", col_perm(axis, RING4[kind][done[p][axis]]))
            sent.append((at, got))
        for p, (at, got) in enumerate(sent):
            axis = PARTS[p][5][step]
            values[p] = lax.index_in_dim(values[p], 0, at, keepdims=False) + got
            dims[p].pop(at)
            done[p][axis] += 1
    return values


def col_total(value):
    value = value + lax.ppermute(value, "col", col_perm("c", 1))
    for axis in "xy":
        value = value + sum(lax.ppermute(value, "col", col_perm(axis, m)) for m in (1, 2, 3))
    return value


def on_device(activations, kv_grads, row_state, col_state):
    z = lax.axis_index("row").astype(jnp.int32)
    col = lax.axis_index("col").astype(jnp.int32)
    xi, yi, ci = col // 8, (col // 2) % 4, col % 2

    step_masks = [(a, b) for a in range(4) for b in range(4)]
    mx = jnp.asarray(np.array([a for a, _ in step_masks], np.int32))
    my = jnp.asarray(np.array([b for _, b in step_masks], np.int32))
    z0 = z ^ jnp.asarray(np.array(masks8(), np.int32))
    z1 = ((((z + 1) % 8) ^ jnp.asarray(np.array(masks8(), np.int32))) + 7) % 8
    slots = [
        np.array([masks4(kind).index(a) * 4 + masks4(kind).index(b) for a, b in step_masks], np.int32)
        for kind in (0, 1)
    ]
    blocks = ((xi ^ mx) * 4 + (yi ^ my)) * 2
    rest = [jnp.zeros((16,), jnp.int32), z0, z1, jnp.asarray(slots[0]), jnp.asarray(slots[1])]
    far = jnp.concatenate([blocks + (1 - ci)] + rest)
    near = jnp.concatenate([blocks + ci] + rest)

    away = partial(far, activations, kv_grads, [])
    came = [lax.ppermute(a, "col", col_perm("c", 1)) for a in away]
    parts = reduce_parts(partial(near, activations, kv_grads, came))
    wide = jnp.concatenate(parts[:4], axis=0)
    narrow = jnp.concatenate(parts[4:], axis=0)
    grad = jnp.concatenate([wide, narrow], axis=1) * (512 * 256) ** (-0.5)

    square = grad * grad
    squares = square + EPSILON
    even = lax.broadcasted_iota(jnp.int32, (1, 512), 1) % 2 == 0
    col_sum = jnp.stack(
        [jnp.sum(jnp.where(even, squares, 0.0), axis=1), jnp.sum(jnp.where(even, 0.0, squares), axis=1)]
    )
    col_old = lax.dynamic_slice_in_dim(col_state, z * 32, 32, axis=1)
    col_part = DECAY_RATE * col_old + (1.0 - DECAY_RATE) * (col_sum / HEAD_DIM)
    of_row = jnp.where(even, col_part[0][:, None], col_part[1][:, None])
    stats = jnp.stack([jnp.sum(squares, axis=0), jnp.sum(square / of_row, axis=0)])
    stats = col_total(stats.reshape(8, 128))

    tile = grad.reshape(2, 16, 8, 64).transpose(2, 1, 0, 3).reshape(8, 16, 128)
    small = jnp.concatenate([col_part.reshape(64), row_state, jnp.zeros((7 * 128,), jnp.float32)]).reshape(8, 128)
    common = jnp.concatenate([stats, small], axis=0)
    load = jnp.concatenate([tile, jnp.broadcast_to(common, (8, 16, 128))], axis=1)
    load = lax.all_to_all(load, "row", 0, 0, tiled=True)

    grad = load[:, :16].reshape(8, 16, 2, 64).transpose(3, 0, 2, 1).reshape(64, 256)
    total = jnp.sum(load[:, 16:24], axis=0).reshape(2, 512)
    col_new = load[:, 24, :64].reshape(8, 2, 32).transpose(1, 0, 2).reshape(2, 256)
    row_old = load[:, 24, 64:].reshape(512)
    row_all = DECAY_RATE * row_old + (1.0 - DECAY_RATE) * (total[0] / D)
    per_row = total[1] / row_all
    clip = jnp.sum(per_row.reshape(256, 2), axis=0)
    limiter = jnp.maximum(1.0, jnp.sqrt(clip / (HEAD_DIM * D)) / CLIP_LIMIT)
    row_new = lax.dynamic_slice_in_dim(row_all, z * 64, 64)
    key_row = lax.broadcasted_iota(jnp.int32, (64, 1), 0) % 2 == 0
    moment = row_new[:, None] * jnp.where(key_row, col_new[0][None, :], col_new[1][None, :])
    direction = grad / jnp.sqrt(moment) / jnp.where(key_row, limiter[0], limiter[1])
    return (direction, row_new, col_new)


def solution(mesh):
    placed = (P(("row", "col"), None), P(("row", "col"), None), P("row"), P(None, "col"))
    return jax.shard_map(
        on_device,
        mesh=mesh,
        in_specs=placed,
        out_specs=(P("row", "col"), P("row"), P(None, "col")),
        check_vma=False,
    )
```

```python
import functools
import jax
import jax.numpy as jnp
from jax import lax
from jax.experimental import pallas as pl
from jax.experimental.pallas import tpu as pltpu
from jax.sharding import PartitionSpec as P

D = 8192
HEAD_DIM = 256
TOKENS = 131072
DECAY_RATE = 1.0 - 8.0 ** (-0.8)
EPSILON = 1e-30
CLIP_LIMIT = 1.0
MIB = 1024 * 1024

RING4 = ((1, 3), (3, 1))
RING8 = (1, 2, 6)
Z_MASKS = [i * RING8[0] ^ j * RING8[1] ^ k * RING8[2] for i in (0, 1) for j in (0, 1) for k in (0, 1)]
UNITS = ((0, 6), (6, 12), (12, 16))


def swap_cores(value):
    return lax.ppermute(value, "col", [(i, i ^ 1) for i in range(32)])


def along(axis, step, value):
    if axis == "z":
        pairs = []
        for z in range(8):
            for i in range(32):
                core = i % 2
                to = ((((z + core) % 8) ^ RING8[step]) + 8 - core) % 8
                pairs.append((z * 32 + i, to * 32 + i))
        return lax.ppermute(value, ("row", "col"), pairs)
    shift = 3 if axis == "x" else 1
    return lax.ppermute(value, "col", [(i, i ^ (RING4[i % 2][step] << shift)) for i in range(32)])


def partial_kernel(chunk, to_sibling, pos, *refs):
    xs, y_ref, acc = refs[:4], refs[4], refs[-1]
    z, core = pos[0], lax.rem(pos[1], 2)
    core = 1 - core if to_sibling else core
    if to_sibling:
        out = refs[5]
    else:
        got = refs[5]
        outs = refs[6:-1]
    starts = [
        pl.multiple_of(lax.rem((lax.rem(z + core, 8) ^ mask) + 8 - core, 8) * 32, 32) for mask in Z_MASKS
    ]
    for s in range(4):
        acc[s] = lax.dot_general(
            xs[s][...], y_ref[...], (((0,), (0,)), ((), ())), preferred_element_type=jnp.float32
        )
        for slot in range(8):
            for unit in range(16):
                group, lane = divmod(unit, 4)
                value = acc[s, pl.ds(starts[slot] + group * 8, 8), lane * 128 : lane * 128 + 128]
                if to_sibling:
                    out[0, s, slot, unit] = value
                    continue
                value = value + got[0, s, slot, unit]
                if unit < 6:
                    outs[0][0, s, slot, unit] = value
                elif unit < 12:
                    outs[1 if s >= 2 else 2][0, s % 2, slot, unit - 6] = value
                else:
                    outs[3 if slot >= 4 else 4][0, s, slot % 4, unit - 12] = value


def partial(pos, x, y, chunk, got=None):
    to_sibling = got is None

    def block(s):
        def index(step, pos):
            core = lax.rem(pos[1], 2)
            core = 1 - core if to_sibling else core
            first, second = 1 + 2 * core, 3 - 2 * core
            xi = lax.div(pos[1], 8) ^ (first * chunk) ^ (second * step)
            yi = lax.rem(lax.div(pos[1], 2), 4) ^ (first * (s // 2)) ^ (second * (s % 2))
            return (0, (xi * 4 + yi) * 2 + core)

        return pl.BlockSpec((512, 256), index)

    def whole(shape):
        return pl.BlockSpec((1,) + shape[1:], lambda step, pos: (step,) + (0,) * (len(shape) - 1))

    full = (2, 4, 8, 16, 8, 128)
    if to_sibling:
        shapes = [full]
    else:
        part_b, part_c = (2, 2, 8, 6, 8, 128), (2, 4, 4, 4, 8, 128)
        shapes = [(2, 4, 8, 6, 8, 128), part_b, part_b, part_c, part_c]
    return pl.pallas_call(
        functools.partial(partial_kernel, chunk, to_sibling),
        grid_spec=pltpu.PrefetchScalarGridSpec(
            num_scalar_prefetch=1,
            grid=(2,),
            in_specs=[block(s) for s in range(4)]
            + [pl.BlockSpec((512, 512), lambda step, pos: (0, 0))]
            + ([] if to_sibling else [whole(full)]),
            out_specs=[whole(s) for s in shapes],
            scratch_shapes=[pltpu.VMEM((4, 256, 512), jnp.float32)],
        ),
        out_shape=[jax.ShapeDtypeStruct(s, jnp.float32) for s in shapes],
        compiler_params=pltpu.CompilerParams(vmem_limit_bytes=56 * MIB),
        cost_estimate=pl.CostEstimate(
            flops=2 * 512 * 512 * 2048, bytes_accessed=(7 if to_sibling else 11) * MIB, transcendentals=0
        ),
        name=("away" if to_sibling else "near") + str(chunk),
    )(pos, x, x, x, x, y, *([] if to_sibling else [got]))


def stats_kernel(pos, units, col_old, row_old, tile, stats):
    z = pos[0]
    lane = lax.broadcasted_iota(jnp.int32, (8, 128), 1)
    sub = lax.broadcasted_iota(jnp.int32, (8, 128), 0)
    even = lane % 2 == 0
    upper = lane >= 64
    scale = float(TOKENS) ** -0.5
    place = 64 + 32 * lax.rem(z, 2)
    col_row = [jnp.zeros((1, 128), jnp.float32)] * 2
    squares_of = [jnp.zeros((1, 128), jnp.float32)] * 4
    raised_of = [jnp.zeros((1, 128), jnp.float32)] * 4
    for group in range(4):
        grads = [units[group * 4 + i] * scale for i in range(4)]
        square = [g * g for g in grads]
        total = sum(s + EPSILON for s in square)
        sums = [
            jnp.sum(jnp.where(even, total, 0.0), axis=1, keepdims=True),
            jnp.sum(jnp.where(even, 0.0, total), axis=1, keepdims=True),
        ]
        factor = []
        for m in range(2):
            old = col_old[group * 8 : group * 8 + 8, m : m + 1]
            new = DECAY_RATE * old + (1.0 - DECAY_RATE) * (sums[m] / HEAD_DIM)
            new = jnp.broadcast_to(new, (8, 128))
            factor.append(new)
            placed = jnp.where(lane == sub + (group * 8 + place), new, 0.0)
            col_row[m] = col_row[m] + jnp.sum(placed, axis=0, keepdims=True)
        inverse = lax.rsqrt(jnp.where(even, factor[0], factor[1]))
        for i in range(4):
            scaled = grads[i] * inverse
            squares_of[i] = squares_of[i] + jnp.sum(square[i] + EPSILON, axis=0, keepdims=True)
            raised_of[i] = raised_of[i] + jnp.sum(scaled * scaled, axis=0, keepdims=True)
            low = jnp.where(upper, 0.0, scaled)
            high = jnp.where(upper, 0.0, pltpu.roll(scaled, 64, 1))
            tile[2 * i, group * 8 : group * 8 + 8] = low
            tile[2 * i + 1, group * 8 : group * 8 + 8] = high
    for base, rows in ((0, squares_of), (8, raised_of)):
        value = jnp.zeros((8, 128), jnp.float32)
        for i in range(4):
            both = jnp.broadcast_to(rows[i], (8, 128))
            value = jnp.where(sub == 2 * i, pltpu.roll(both, 64, 1), value)
            value = jnp.where(sub == 2 * i + 1, both, value)
        stats[base : base + 8] = jnp.where(upper, value, 0.0)
    olds = jnp.where((sub == z) & upper, jnp.broadcast_to(row_old[...], (8, 128)), 0.0)
    cols = jnp.zeros((8, 128), jnp.float32)
    for m in range(2):
        cols = jnp.where(sub == 4 * m + lax.div(z, 2), jnp.broadcast_to(col_row[m], (8, 128)), cols)
    for to in range(8):
        tile[to, 16:24] = tile[to, 16:24] + olds
        tile[to, 24:32] = tile[to, 24:32] + cols


def finish_kernel(pos, load, direction, row_new, col_new, scales, rows):
    z = pos[0]
    lane = lax.broadcasted_iota(jnp.int32, (8, 128), 1)
    even = lane % 2 == 0
    upper = lane >= 64
    total = load[0]
    for i in range(1, 8):
        total = total + load[i]
    row_all = DECAY_RATE * total[16:24] + (1.0 - DECAY_RATE) * (total[0:8] / D)
    row_all = jnp.where(upper, row_all, 1.0)
    per_row = jnp.where(upper, total[8:16] / row_all, 0.0)
    limiter = []
    for keep in (even, jnp.logical_not(even)):
        clip = jnp.sum(jnp.where(keep, per_row, 0.0), axis=(0, 1), keepdims=True)
        limiter.append(jnp.maximum(1.0, jnp.sqrt(clip / (HEAD_DIM * D)) / CLIP_LIMIT))
    bound = jnp.where(even, jnp.broadcast_to(limiter[0], (8, 128)), jnp.broadcast_to(limiter[1], (8, 128)))
    scales[...] = pltpu.roll(lax.rsqrt(row_all) / bound, 64, 1)
    rows[...] = pltpu.roll(row_all, 64, 1)
    row_new[...] = rows[pl.ds(z, 1), 0:64]
    mine = jnp.broadcast_to(scales[pl.ds(z, 1), :], (128, 128))
    for half in range(2):
        block = jnp.concatenate([load[4 * half + i] for i in range(4)], axis=0) * mine
        direction[:, half * 128 : half * 128 + 128] = block.T[0:64]
    cols = total[24:32]
    moved = pltpu.roll(cols, 64, 1)
    for m in range(2):
        for half in range(2):
            at = 4 * m + 2 * half
            pair = jnp.where(upper[0:1], cols[at + 1 : at + 2], moved[at : at + 1])
            col_new[m : m + 1, half * 128 : half * 128 + 128] = pair


def on_device(activations, kv_grads, row_state, col_state):
    z = lax.axis_index("row").astype(jnp.int32)
    pos = jnp.stack([z, lax.axis_index("col").astype(jnp.int32)])
    col_old = lax.dynamic_slice_in_dim(col_state, z * 32, 32, axis=1).T
    row_old = jnp.concatenate([row_state, row_state]).reshape(1, 128)

    sent = [swap_cores(partial(pos, activations, kv_grads, chunk)[0]) for chunk in (1, 0)]
    a_send, b_send1, b_keep1, c_send1, c_keep1 = partial(pos, activations, kv_grads, 1, sent[0])
    a_keep, b_send0, b_keep0, c_send0, c_keep0 = partial(pos, activations, kv_grads, 0, sent[1])

    got = along("x", 0, a_send), along("y", 0, b_send1), along("z", 0, c_send1)
    got = got + (along("y", 0, b_send0), along("z", 0, c_send0))
    got = lax.optimization_barrier(got)
    a = (a_keep + got[0]).reshape(2, 2, 2, 2, 2, 2, 6, 8, 128)
    b1 = (b_keep1 + got[1]).reshape(2, 2, 2, 2, 2, 6, 8, 128)
    b0 = (b_keep0 + got[3]).reshape(2, 2, 2, 2, 2, 6, 8, 128)
    c1 = (c_keep1 + got[2]).reshape(2, 2, 2, 2, 2, 4, 8, 128)
    c0 = (c_keep0 + got[4]).reshape(2, 2, 2, 2, 2, 4, 8, 128)

    got = along("y", 0, a[:, 1]), along("z", 0, jnp.stack([b1[:, :, 1], b0[:, :, 1]])), along("x", 0, c1)
    got = lax.optimization_barrier(got)
    a = a[:, 0] + got[0]
    b1, b0 = b1[:, :, 0] + got[1][0], b0[:, :, 0] + got[1][1]
    c = c0 + got[2]

    got = along("z", 0, a[:, :, 1]), along("x", 0, b1), along("y", 0, c[:, 1])
    got = lax.optimization_barrier(got)
    a = a[:, :, 0] + got[0]
    b = b0 + got[1]
    c = c[:, 0] + got[2]

    value = jnp.concatenate([a, b, c], axis=4)
    for axis, step in (("x", 1), ("y", 1), ("z", 1), ("z", 2)):
        value = value[0] + along(axis, step, value[1])

    tile, stats = pl.pallas_call(
        stats_kernel,
        in_specs=[pl.BlockSpec(memory_space=pltpu.SMEM)] + [pl.BlockSpec(memory_space=pltpu.VMEM)] * 3,
        out_specs=[pl.BlockSpec(memory_space=pltpu.VMEM)] * 2,
        out_shape=[
            jax.ShapeDtypeStruct((8, 32, 128), jnp.float32),
            jax.ShapeDtypeStruct((16, 128), jnp.float32),
        ],
        name="stats",
    )(pos, value, col_old, row_old)

    stats = stats + swap_cores(stats)
    for shift in (3, 1):
        others = [lax.ppermute(stats, "col", [(i, i ^ (m << shift)) for i in range(32)]) for m in (1, 2, 3)]
        stats = stats + others[0] + others[1] + others[2]
    load = jnp.concatenate([tile[:, :16] + stats[None], tile[:, 16:]], axis=1)
    load = lax.all_to_all(load, "row", 0, 0, tiled=True)

    direction, row_new, col_new = pl.pallas_call(
        finish_kernel,
        in_specs=[pl.BlockSpec(memory_space=pltpu.SMEM), pl.BlockSpec(memory_space=pltpu.VMEM)],
        out_specs=[pl.BlockSpec(memory_space=pltpu.VMEM)] * 3,
        out_shape=[
            jax.ShapeDtypeStruct((64, 256), jnp.float32),
            jax.ShapeDtypeStruct((1, 64), jnp.float32),
            jax.ShapeDtypeStruct((2, 256), jnp.float32),
        ],
        scratch_shapes=[pltpu.VMEM((8, 128), jnp.float32)] * 2,
        name="finish",
    )(pos, load)
    return (direction, row_new.reshape(64), col_new)


def solution(mesh):
    placed = (P(("row", "col"), None), P(("row", "col"), None), P("row"), P(None, "col"))
    return jax.shard_map(
        on_device,
        mesh=mesh,
        in_specs=placed,
        out_specs=(P("row", "col"), P("row"), P(None, "col")),
        check_vma=False,
    )
```

```python
import functools
import jax
import jax.numpy as jnp
from jax import lax
from jax.experimental import pallas as pl
from jax.experimental.pallas import tpu as pltpu
from jax.sharding import PartitionSpec as P

D = 8192
HEAD_DIM = 256
TOKENS = 131072
DECAY_RATE = 1.0 - 8.0 ** (-0.8)
EPSILON = 1e-30
CLIP_LIMIT = 1.0
MIB = 1024 * 1024
GRANTS = (52, 44, 20, 20)

RING4 = ((1, 3), (3, 1))
RING8 = (1, 2, 6)
Z_MASKS = [i * RING8[0] ^ j * RING8[1] ^ k * RING8[2] for i in (0, 1) for j in (0, 1) for k in (0, 1)]
UNITS = ((0, 6), (6, 11), (11, 16))


def swap_cores(value):
    return lax.ppermute(value, "col", [(i, i ^ 1) for i in range(32)])


def along(axis, step, value):
    if axis == "z":
        pairs = []
        for z in range(8):
            for i in range(32):
                core = i % 2
                to = ((((z + core) % 8) ^ RING8[step]) + 8 - core) % 8
                pairs.append((z * 32 + i, to * 32 + i))
        return lax.ppermute(value, ("row", "col"), pairs)
    unit = sum({"x": 8, "y": 2}[name] for name in axis)
    return lax.ppermute(value, "col", [(i, i ^ (RING4[i % 2][step] * unit)) for i in range(32)])


def partial_kernel(chunk, to_sibling, pos, *refs):
    step = pl.program_id(0)
    z, core = pos[0], lax.rem(pos[1], 2)
    core = 1 - core if to_sibling else core
    xs, y = refs[:4], refs[4]
    if to_sibling:
        full = refs[5]
    else:
        got, a, b_send, b_keep, c = refs[5:]
    slots = []
    for place in range(8):
        mask = lax.rem(place + core, 8) ^ lax.rem(z + core, 8)
        high = lax.div(mask, 4)
        slots.append(lax.rem(mask, 2) * 4 + (lax.rem(lax.div(mask, 2), 2) ^ high) * 2 + high)
    for s in range(4):
        value = lax.dot_general(
            xs[s][...], y[...], (((0,), (0,)), ((), ())), preferred_element_type=jnp.float32
        )
        for place, slot in enumerate(slots):
            for unit in range(16):
                group, lane = divmod(unit, 4)
                top = place * 32 + group * 8
                piece = value[top : top + 8, lane * 128 : lane * 128 + 128]
                if to_sibling:
                    full[step, s, slot, unit] = piece
                    continue
                piece = piece + got[step, s, slot, unit]
                if unit < UNITS[0][1]:
                    a[step, s, slot, unit] = piece
                elif unit < UNITS[1][1]:
                    (b_send if s >= 2 else b_keep)[step, s % 2, slot, unit - UNITS[1][0]] = piece
                else:
                    c[step, s, slot, unit - UNITS[2][0]] = piece


def partial(pos, x, y, chunk, grant, got=None):
    to_sibling = got is None
    na, nb, nc = (to - start for start, to in UNITS)

    def block(s):
        def index(step, pos):
            core = lax.rem(pos[1], 2)
            core = 1 - core if to_sibling else core
            first, second = 1 + 2 * core, 3 - 2 * core
            xi = lax.div(pos[1], 8) ^ (first * chunk) ^ (second * step)
            yi = lax.rem(lax.div(pos[1], 2), 4) ^ (first * (s // 2)) ^ (second * (s % 2))
            return (0, (xi * 4 + yi) * 2 + core)

        return pl.BlockSpec((512, 256), index)

    if to_sibling:
        shapes = [(2, 4, 8, 16, 8, 128)]
    else:
        part_b, part_c = (2, 2, 8, nb, 8, 128), (2, 4, 8, nc, 8, 128)
        shapes = [(2, 4, 8, na, 8, 128), part_b, part_b, part_c]
    whole = pl.BlockSpec(memory_space=pltpu.VMEM)
    return pl.pallas_call(
        functools.partial(partial_kernel, chunk, to_sibling),
        grid_spec=pltpu.PrefetchScalarGridSpec(
            num_scalar_prefetch=1,
            grid=(2,),
            in_specs=[block(s) for s in range(4)]
            + [pl.BlockSpec((512, 512), lambda step, pos: (0, 0))]
            + ([] if to_sibling else [whole]),
            out_specs=[whole] * len(shapes),
        ),
        out_shape=[pltpu.VMEM(s, jnp.float32) for s in shapes],
        compiler_params=pltpu.CompilerParams(vmem_limit_bytes=grant * MIB),
        cost_estimate=pl.CostEstimate(
            flops=2 * 512 * 512 * 2048, bytes_accessed=(7 if to_sibling else 11) * MIB, transcendentals=0
        ),
        name=("away" if to_sibling else "near") + str(chunk),
    )(pos, x, x, x, x, y, *([] if to_sibling else [got]))


def stats_kernel(pos, units, col_old, row_old, tile, stats):
    z = pos[0]
    lane = lax.broadcasted_iota(jnp.int32, (8, 128), 1)
    sub = lax.broadcasted_iota(jnp.int32, (8, 128), 0)
    even = lane % 2 == 0
    upper = lane >= 64
    scale = float(TOKENS) ** -0.5
    place = 64 + 32 * lax.rem(z, 2)
    col_row = [jnp.zeros((1, 128), jnp.float32)] * 2
    squares_of = [jnp.zeros((1, 128), jnp.float32)] * 4
    raised_of = [jnp.zeros((1, 128), jnp.float32)] * 4
    for group in range(4):
        grads = [units[group * 4 + i] * scale for i in range(4)]
        square = [g * g for g in grads]
        total = sum(s + EPSILON for s in square)
        sums = [
            jnp.sum(jnp.where(even, total, 0.0), axis=1, keepdims=True),
            jnp.sum(jnp.where(even, 0.0, total), axis=1, keepdims=True),
        ]
        factor = []
        for m in range(2):
            old = col_old[group * 8 : group * 8 + 8, m : m + 1]
            new = DECAY_RATE * old + (1.0 - DECAY_RATE) * (sums[m] / HEAD_DIM)
            new = jnp.broadcast_to(new, (8, 128))
            factor.append(new)
            placed = jnp.where(lane == sub + (group * 8 + place), new, 0.0)
            col_row[m] = col_row[m] + jnp.sum(placed, axis=0, keepdims=True)
        inverse = lax.rsqrt(jnp.where(even, factor[0], factor[1]))
        for i in range(4):
            scaled = grads[i] * inverse
            squares_of[i] = squares_of[i] + jnp.sum(square[i] + EPSILON, axis=0, keepdims=True)
            raised_of[i] = raised_of[i] + jnp.sum(scaled * scaled, axis=0, keepdims=True)
            low = jnp.where(upper, 0.0, scaled)
            high = jnp.where(upper, 0.0, pltpu.roll(scaled, 64, 1))
            tile[2 * i, group * 8 : group * 8 + 8] = low
            tile[2 * i + 1, group * 8 : group * 8 + 8] = high
    value = jnp.zeros((8, 128), jnp.float32)
    for i, row in enumerate(squares_of + raised_of):
        value = jnp.where(sub == i, jnp.broadcast_to(row, (8, 128)), value)
    for to in range(32):
        stats[to] = value
    olds = jnp.where((sub == z) & upper, jnp.broadcast_to(row_old[...], (8, 128)), 0.0)
    cols = jnp.zeros((8, 128), jnp.float32)
    for m in range(2):
        cols = jnp.where(sub == 4 * m + lax.div(z, 2), jnp.broadcast_to(col_row[m], (8, 128)), cols)
    for to in range(8):
        tile[to, 16:24] = tile[to, 16:24] + olds
        tile[to, 24:32] = tile[to, 24:32] + cols


def pack_kernel(tile, stats, load):
    sub = lax.broadcasted_iota(jnp.int32, (8, 128), 0)
    upper = lax.broadcasted_iota(jnp.int32, (8, 128), 1) >= 64
    sums = [stats[i] for i in range(32)]
    while len(sums) > 1:
        sums = [p + q for p, q in zip(sums[::2], sums[1::2])]
    placed = []
    for base in (0, 4):
        value = jnp.zeros((8, 128), jnp.float32)
        for i in range(4):
            both = jnp.broadcast_to(sums[0][base + i : base + i + 1], (8, 128))
            value = jnp.where(sub == 2 * i, pltpu.roll(both, 64, 1), value)
            value = jnp.where(sub == 2 * i + 1, both, value)
        placed.append(jnp.where(upper, value, 0.0))
    for to in range(8):
        load[to, 0:8] = tile[to, 0:8] + placed[0]
        load[to, 8:16] = tile[to, 8:16] + placed[1]
        load[to, 16:32] = tile[to, 16:32]


def finish_kernel(pos, load, direction, row_new, col_new, scales, rows):
    z = pos[0]
    lane = lax.broadcasted_iota(jnp.int32, (8, 128), 1)
    even = lane % 2 == 0
    upper = lane >= 64
    total = load[0]
    for i in range(1, 8):
        total = total + load[i]
    row_all = DECAY_RATE * total[16:24] + (1.0 - DECAY_RATE) * (total[0:8] / D)
    row_all = jnp.where(upper, row_all, 1.0)
    per_row = jnp.where(upper, total[8:16] / row_all, 0.0)
    limiter = []
    for keep in (even, jnp.logical_not(even)):
        clip = jnp.sum(jnp.where(keep, per_row, 0.0), axis=(0, 1), keepdims=True)
        limiter.append(jnp.maximum(1.0, jnp.sqrt(clip / (HEAD_DIM * D)) / CLIP_LIMIT))
    bound = jnp.where(even, jnp.broadcast_to(limiter[0], (8, 128)), jnp.broadcast_to(limiter[1], (8, 128)))
    scales[...] = pltpu.roll(lax.rsqrt(row_all) / bound, 64, 1)
    rows[...] = pltpu.roll(row_all, 64, 1)
    row_new[...] = rows[pl.ds(z, 1), 0:64]
    mine = jnp.broadcast_to(scales[pl.ds(z, 1), :], (128, 128))
    for half in range(2):
        block = jnp.concatenate([load[4 * half + i] for i in range(4)], axis=0) * mine
        direction[:, half * 128 : half * 128 + 128] = block.T[0:64]
    cols = total[24:32]
    moved = pltpu.roll(cols, 64, 1)
    for m in range(2):
        for half in range(2):
            at = 4 * m + 2 * half
            pair = jnp.where(upper[0:1], cols[at + 1 : at + 2], moved[at : at + 1])
            col_new[m : m + 1, half * 128 : half * 128 + 128] = pair


def on_device(activations, kv_grads, row_state, col_state):
    z = lax.axis_index("row").astype(jnp.int32)
    pos = jnp.stack([z, lax.axis_index("col").astype(jnp.int32)])
    col_old = lax.dynamic_slice_in_dim(col_state, z * 32, 32, axis=1).T
    row_old = jnp.concatenate([row_state, row_state]).reshape(1, 128)

    x, y = activations, kv_grads
    sent1 = swap_cores(partial(pos, x, y, 1, GRANTS[0])[0])
    sent0 = swap_cores(partial(pos, x, y, 0, GRANTS[1])[0])
    a_send, b_send1, b_keep1, c1 = partial(pos, x, y, 1, GRANTS[2], sent1)
    a_keep, b_send0, b_keep0, c0 = partial(pos, x, y, 0, GRANTS[3], sent0)
    c_send1, c_keep1, c_send0, c_keep0 = c1[:, :, 4:], c1[:, :, :4], c0[:, :, 4:], c0[:, :, :4]

    na, nb, nc = (to - start for start, to in UNITS)
    got = along("x", 0, a_send), along("y", 0, b_send1), along("z", 0, c_send1)
    got = got + (along("y", 0, b_send0), along("z", 0, c_send0))
    ga, gb1, gc1, gb0, gc0 = lax.optimization_barrier(got)
    a, ga = (v.reshape(2, 2, 2, 2, 2, 2, na, 8, 128) for v in (a_keep, ga))
    b1, b0, gb1, gb0 = (v.reshape(2, 2, 2, 2, 2, nb, 8, 128) for v in (b_keep1, b_keep0, gb1, gb0))
    c1, c0, gc1, gc0 = (v.reshape(2, 2, 2, 2, 2, nc, 8, 128) for v in (c_keep1, c_keep0, gc1, gc0))

    a_send = a[:, 1] + ga[:, 1]
    b_send = jnp.stack([b1[:, :, 1] + gb1[:, :, 1], b0[:, :, 1] + gb0[:, :, 1]])
    got = along("y", 0, a_send), along("z", 0, b_send), along("x", 0, c1 + gc1)
    a = a[:, 0] + ga[:, 0]
    b1, b0 = b1[:, :, 0] + gb1[:, :, 0], b0[:, :, 0] + gb0[:, :, 0]
    c = c0 + gc0
    ga, gb, gc = lax.optimization_barrier(got)

    a_send = a[:, :, 1] + ga[:, :, 1]
    got = along("z", 0, a_send), along("x", 0, b1 + gb[0]), along("y", 0, c[:, 1] + gc[:, 1])
    a = a[:, :, 0] + ga[:, :, 0]
    b = b0 + gb[1]
    c = c[:, 0] + gc[:, 0]
    ga, gb, gc = lax.optimization_barrier(got)

    def quarter(i, j):
        return jnp.concatenate([v[i, j] + g[i, j] for v, g in ((a, ga), (b, gb), (c, gc))], axis=2)

    got = along("xy", 1, quarter(1, 1)), along("x", 1, quarter(1, 0)), along("y", 1, quarter(0, 1))
    value = quarter(0, 0) + got[0] + got[1] + got[2]
    for step in (1, 2):
        value = value[0] + along("z", step, value[1])

    tile, stats = pl.pallas_call(
        stats_kernel,
        in_specs=[pl.BlockSpec(memory_space=pltpu.SMEM)] + [pl.BlockSpec(memory_space=pltpu.VMEM)] * 3,
        out_specs=[pl.BlockSpec(memory_space=pltpu.VMEM)] * 2,
        out_shape=[
            jax.ShapeDtypeStruct((8, 32, 128), jnp.float32),
            jax.ShapeDtypeStruct((32, 8, 128), jnp.float32),
        ],
        name="stats",
    )(pos, value, col_old, row_old)

    stats = lax.all_to_all(stats, "col", 0, 0, tiled=True)
    load = pl.pallas_call(
        pack_kernel,
        in_specs=[pl.BlockSpec(memory_space=pltpu.VMEM)] * 2,
        out_specs=pl.BlockSpec(memory_space=pltpu.VMEM),
        out_shape=jax.ShapeDtypeStruct((8, 32, 128), jnp.float32),
        name="pack",
    )(tile, stats)
    load = lax.all_to_all(load, "row", 0, 0, tiled=True)

    direction, row_new, col_new = pl.pallas_call(
        finish_kernel,
        in_specs=[pl.BlockSpec(memory_space=pltpu.SMEM), pl.BlockSpec(memory_space=pltpu.VMEM)],
        out_specs=[pl.BlockSpec(memory_space=pltpu.VMEM)] * 3,
        out_shape=[
            jax.ShapeDtypeStruct((64, 256), jnp.float32),
            jax.ShapeDtypeStruct((1, 64), jnp.float32),
            jax.ShapeDtypeStruct((2, 256), jnp.float32),
        ],
        scratch_shapes=[pltpu.VMEM((8, 128), jnp.float32)] * 2,
        name="finish",
    )(pos, load)
    return (direction, row_new.reshape(64), col_new)


def solution(mesh):
    placed = (P(("row", "col"), None), P(("row", "col"), None), P("row"), P(None, "col"))
    return jax.shard_map(
        on_device,
        mesh=mesh,
        in_specs=placed,
        out_specs=(P("row", "col"), P("row"), P(None, "col")),
        check_vma=False,
    )
```

```python
import functools
import jax
import jax.numpy as jnp
from jax import lax
from jax.experimental import pallas as pl
from jax.experimental.pallas import tpu as pltpu
from jax.sharding import PartitionSpec as P

D = 8192
HEAD_DIM = 256
TOKENS = 131072
DECAY_RATE = 1.0 - 8.0 ** (-0.8)
EPSILON = 1e-30
CLIP_LIMIT = 1.0
MIB = 1024 * 1024
SMALL = pltpu.CompilerParams(vmem_limit_bytes=4 * MIB)
GRANTS = (52, 44, 20, 20)

RING4 = ((1, 3), (3, 1))
RING8 = (1, 2, 6)
Z_MASKS = [i * RING8[0] ^ j * RING8[1] ^ k * RING8[2] for i in (0, 1) for j in (0, 1) for k in (0, 1)]
UNITS = ((0, 6), (6, 11), (11, 16))


def swap_cores(value):
    return lax.ppermute(value, "col", [(i, i ^ 1) for i in range(32)])


def along(axis, step, value):
    if axis == "z":
        pairs = []
        for z in range(8):
            for i in range(32):
                core = i % 2
                to = ((((z + core) % 8) ^ RING8[step]) + 8 - core) % 8
                pairs.append((z * 32 + i, to * 32 + i))
        return lax.ppermute(value, ("row", "col"), pairs)
    unit = sum({"x": 8, "y": 2}[name] for name in axis)
    return lax.ppermute(value, "col", [(i, i ^ (RING4[i % 2][step] * unit)) for i in range(32)])


def partial_kernel(chunk, to_sibling, pos, *refs):
    bit = 1 - pl.program_id(0)
    z, core = pos[0], lax.rem(pos[1], 2)
    core = 1 - core if to_sibling else core
    xs, y = refs[:4], refs[4]
    if to_sibling:
        full = refs[5]
    else:
        got, a, b_send, b_keep, c = refs[5:]
    slots = []
    for place in range(8):
        mask = lax.rem(place + core, 8) ^ lax.rem(z + core, 8)
        high = lax.div(mask, 4)
        slots.append(lax.rem(mask, 2) * 4 + (lax.rem(lax.div(mask, 2), 2) ^ high) * 2 + high)
    for s in range(4):
        value = lax.dot_general(
            xs[s][...], y[...], (((0,), (0,)), ((), ())), preferred_element_type=jnp.float32
        )
        for place, slot in enumerate(slots):
            for unit in range(16):
                group, lane = divmod(unit, 4)
                top = place * 32 + group * 8
                piece = value[top : top + 8, lane * 128 : lane * 128 + 128]
                if to_sibling:
                    full[bit, s, slot, unit] = piece
                    continue
                piece = piece + got[bit, s, slot, unit]
                if unit < UNITS[0][1]:
                    a[bit, s, slot, unit] = piece
                elif unit < UNITS[1][1]:
                    (b_send if s >= 2 else b_keep)[bit, s % 2, slot, unit - UNITS[1][0]] = piece
                else:
                    c[bit, s, slot, unit - UNITS[2][0]] = piece


def partial(pos, x, y, chunk, grant, got=None):
    to_sibling = got is None
    na, nb, nc = (to - start for start, to in UNITS)

    def block(s):
        def index(step, pos):
            core = lax.rem(pos[1], 2)
            core = 1 - core if to_sibling else core
            first, second = 1 + 2 * core, 3 - 2 * core
            xi = lax.div(pos[1], 8) ^ (first * (1 - step)) ^ (second * chunk)
            yi = lax.rem(lax.div(pos[1], 2), 4) ^ (first * (s // 2)) ^ (second * (s % 2))
            return (0, (xi * 4 + yi) * 2 + core)

        return pl.BlockSpec((512, 256), index)

    if to_sibling:
        shapes = [(2, 4, 8, 16, 8, 128)]
    else:
        part_b, part_c = (2, 2, 8, nb, 8, 128), (2, 4, 8, nc, 8, 128)
        shapes = [(2, 4, 8, na, 8, 128), part_b, part_b, part_c]
    whole = pl.BlockSpec(memory_space=pltpu.VMEM)
    return pl.pallas_call(
        functools.partial(partial_kernel, chunk, to_sibling),
        grid_spec=pltpu.PrefetchScalarGridSpec(
            num_scalar_prefetch=1,
            grid=(2,),
            in_specs=[block(s) for s in range(4)]
            + [pl.BlockSpec((512, 512), lambda step, pos: (0, 0))]
            + ([] if to_sibling else [whole]),
            out_specs=[whole] * len(shapes),
        ),
        out_shape=[pltpu.VMEM(s, jnp.float32) for s in shapes],
        compiler_params=pltpu.CompilerParams(vmem_limit_bytes=grant * MIB),
        cost_estimate=pl.CostEstimate(
            flops=2 * 512 * 512 * 2048, bytes_accessed=(7 if to_sibling else 11) * MIB, transcendentals=0
        ),
        name=("away" if to_sibling else "near") + str(chunk),
    )(pos, x, x, x, x, y, *([] if to_sibling else [got]))


def stats_kernel(pos, units, col_old, row_old, tile, stats):
    z = pos[0]
    lane = lax.broadcasted_iota(jnp.int32, (8, 128), 1)
    sub = lax.broadcasted_iota(jnp.int32, (8, 128), 0)
    even = lane % 2 == 0
    upper = lane >= 64
    scale = float(TOKENS) ** -0.5
    place = 64 + 32 * lax.rem(z, 2)
    col_row = [jnp.zeros((1, 128), jnp.float32)] * 2
    squares_of = [jnp.zeros((1, 128), jnp.float32)] * 4
    raised_of = [jnp.zeros((1, 128), jnp.float32)] * 4
    for group in range(4):
        grads = [units[group * 4 + i] * scale for i in range(4)]
        square = [g * g for g in grads]
        total = sum(s + EPSILON for s in square)
        sums = [
            jnp.sum(jnp.where(even, total, 0.0), axis=1, keepdims=True),
            jnp.sum(jnp.where(even, 0.0, total), axis=1, keepdims=True),
        ]
        factor = []
        for m in range(2):
            old = col_old[group * 8 : group * 8 + 8, m : m + 1]
            new = DECAY_RATE * old + (1.0 - DECAY_RATE) * (sums[m] / HEAD_DIM)
            new = jnp.broadcast_to(new, (8, 128))
            factor.append(new)
            placed = jnp.where(lane == sub + (group * 8 + place), new, 0.0)
            col_row[m] = col_row[m] + jnp.sum(placed, axis=0, keepdims=True)
        inverse = lax.rsqrt(jnp.where(even, factor[0], factor[1]))
        for i in range(4):
            scaled = grads[i] * inverse
            squares_of[i] = squares_of[i] + jnp.sum(square[i] + EPSILON, axis=0, keepdims=True)
            raised_of[i] = raised_of[i] + jnp.sum(scaled * scaled, axis=0, keepdims=True)
            low = jnp.where(upper, 0.0, scaled)
            high = jnp.where(upper, 0.0, pltpu.roll(scaled, 64, 1))
            tile[2 * i, group * 8 : group * 8 + 8] = low
            tile[2 * i + 1, group * 8 : group * 8 + 8] = high
    value = jnp.zeros((8, 128), jnp.float32)
    for i, row in enumerate(squares_of + raised_of):
        value = jnp.where(sub == i, jnp.broadcast_to(row, (8, 128)), value)
    for to in range(32):
        stats[to] = value
    olds = jnp.where((sub == z) & upper, jnp.broadcast_to(row_old[...], (8, 128)), 0.0)
    cols = jnp.zeros((8, 128), jnp.float32)
    for m in range(2):
        cols = jnp.where(sub == 4 * m + lax.div(z, 2), jnp.broadcast_to(col_row[m], (8, 128)), cols)
    for to in range(8):
        tile[to, 16:24] = tile[to, 16:24] + olds
        tile[to, 24:32] = tile[to, 24:32] + cols


def pack_kernel(tile, stats, load):
    sub = lax.broadcasted_iota(jnp.int32, (8, 128), 0)
    upper = lax.broadcasted_iota(jnp.int32, (8, 128), 1) >= 64
    sums = [stats[i] for i in range(32)]
    while len(sums) > 1:
        sums = [p + q for p, q in zip(sums[::2], sums[1::2])]
    placed = []
    for base in (0, 4):
        value = jnp.zeros((8, 128), jnp.float32)
        for i in range(4):
            both = jnp.broadcast_to(sums[0][base + i : base + i + 1], (8, 128))
            value = jnp.where(sub == 2 * i, pltpu.roll(both, 64, 1), value)
            value = jnp.where(sub == 2 * i + 1, both, value)
        placed.append(jnp.where(upper, value, 0.0))
    for to in range(8):
        load[to, 0:8] = tile[to, 0:8] + placed[0]
        load[to, 8:16] = tile[to, 8:16] + placed[1]
        load[to, 16:32] = tile[to, 16:32]


def finish_kernel(pos, load, direction, row_new, col_new, scales, rows):
    z = pos[0]
    lane = lax.broadcasted_iota(jnp.int32, (8, 128), 1)
    even = lane % 2 == 0
    upper = lane >= 64
    total = load[0]
    for i in range(1, 8):
        total = total + load[i]
    row_all = DECAY_RATE * total[16:24] + (1.0 - DECAY_RATE) * (total[0:8] / D)
    row_all = jnp.where(upper, row_all, 1.0)
    per_row = jnp.where(upper, total[8:16] / row_all, 0.0)
    limiter = []
    for keep in (even, jnp.logical_not(even)):
        clip = jnp.sum(jnp.where(keep, per_row, 0.0), axis=(0, 1), keepdims=True)
        limiter.append(jnp.maximum(1.0, jnp.sqrt(clip / (HEAD_DIM * D)) / CLIP_LIMIT))
    bound = jnp.where(even, jnp.broadcast_to(limiter[0], (8, 128)), jnp.broadcast_to(limiter[1], (8, 128)))
    scales[...] = pltpu.roll(lax.rsqrt(row_all) / bound, 64, 1)
    rows[...] = pltpu.roll(row_all, 64, 1)
    row_new[...] = rows[pl.ds(z, 1), 0:64]
    mine = jnp.broadcast_to(scales[pl.ds(z, 1), :], (128, 128))
    for half in range(2):
        block = jnp.concatenate([load[4 * half + i] for i in range(4)], axis=0) * mine
        direction[:, half * 128 : half * 128 + 128] = block.T[0:64]
    cols = total[24:32]
    moved = pltpu.roll(cols, 64, 1)
    for m in range(2):
        for half in range(2):
            at = 4 * m + 2 * half
            pair = jnp.where(upper[0:1], cols[at + 1 : at + 2], moved[at : at + 1])
            col_new[m : m + 1, half * 128 : half * 128 + 128] = pair


def on_device(activations, kv_grads, row_state, col_state):
    z = lax.axis_index("row").astype(jnp.int32)
    pos = jnp.stack([z, lax.axis_index("col").astype(jnp.int32)])
    col_old = lax.dynamic_slice_in_dim(col_state, z * 32, 32, axis=1).T
    row_old = jnp.concatenate([row_state, row_state]).reshape(1, 128)

    x, y = activations, kv_grads
    na, nb, nc = (to - start for start, to in UNITS)
    sent = [swap_cores(partial(pos, x, y, 1 - i, GRANTS[i])[0]) for i in (0, 1)]
    streams = [None, None]
    for i in (0, 1):
        a, b_send, b_keep, c = partial(pos, x, y, 1 - i, GRANTS[2 + i], sent[i])
        a = a.reshape(2, 2, 2, 2, 2, 2, na, 8, 128)
        b_send, b_keep = (v.reshape(2, 2, 2, 2, 2, nb, 8, 128) for v in (b_send, b_keep))
        c = c.reshape(2, 2, 2, 2, 2, 2, nc, 8, 128)

        got = along("x", 0, a[1]), along("y", 0, b_send), along("z", 0, c[:, :, :, 1])
        a, b, c = a[0], b_keep, c[:, :, :, 0]
        ga, gb, gc = lax.optimization_barrier(got)

        a_send, b_send, c_send = a[1] + ga[1], b[:, :, 1] + gb[:, :, 1], c[1] + gc[1]
        got = along("y", 0, a_send), along("z", 0, b_send), along("x", 0, c_send)
        a, b, c = a[0] + ga[0], b[:, :, 0] + gb[:, :, 0], c[0] + gc[0]
        ga, gb, gc = lax.optimization_barrier(got)

        a_send, b_send, c_send = a[:, 1] + ga[:, 1], b[1] + gb[1], c[1] + gc[1]
        got = along("z", 0, a_send), along("x", 0, b_send), along("y", 0, c_send)
        a, b, c = a[:, 0] + ga[:, 0], b[0] + gb[0], c[0] + gc[0]
        ga, gb, gc = lax.optimization_barrier(got)
        streams[1 - i] = ((a, ga), (b, gb), (c, gc))

    def quarter(i, j):
        return jnp.concatenate([v[j] + g[j] for v, g in streams[i]], axis=2)

    got = along("xy", 1, quarter(1, 1)), along("x", 1, quarter(1, 0)), along("y", 1, quarter(0, 1))
    value = quarter(0, 0) + got[0] + got[1] + got[2]
    for step in (1, 2):
        value = value[0] + along("z", step, value[1])

    tile, stats = pl.pallas_call(
        stats_kernel,
        in_specs=[pl.BlockSpec(memory_space=pltpu.SMEM)] + [pl.BlockSpec(memory_space=pltpu.VMEM)] * 3,
        out_specs=[pl.BlockSpec(memory_space=pltpu.VMEM)] * 2,
        out_shape=[
            pltpu.VMEM((8, 32, 128), jnp.float32),
            pltpu.VMEM((32, 8, 128), jnp.float32),
        ],
        compiler_params=SMALL,
        name="stats",
    )(pos, value, col_old, row_old)

    stats = lax.all_to_all(stats, "col", 0, 0, tiled=True)
    load = pl.pallas_call(
        pack_kernel,
        in_specs=[pl.BlockSpec(memory_space=pltpu.VMEM)] * 2,
        out_specs=pl.BlockSpec(memory_space=pltpu.VMEM),
        out_shape=pltpu.VMEM((8, 32, 128), jnp.float32),
        compiler_params=SMALL,
        name="pack",
    )(tile, stats)
    load = lax.all_to_all(load, "row", 0, 0, tiled=True)

    direction, row_new, col_new = pl.pallas_call(
        finish_kernel,
        in_specs=[pl.BlockSpec(memory_space=pltpu.SMEM), pl.BlockSpec(memory_space=pltpu.VMEM)],
        out_specs=[pl.BlockSpec(memory_space=pltpu.VMEM)] * 3,
        out_shape=[
            jax.ShapeDtypeStruct((64, 256), jnp.float32),
            jax.ShapeDtypeStruct((1, 64), jnp.float32),
            jax.ShapeDtypeStruct((2, 256), jnp.float32),
        ],
        scratch_shapes=[pltpu.VMEM((8, 128), jnp.float32)] * 2,
        compiler_params=SMALL,
        name="finish",
    )(pos, load)
    return (direction, row_new.reshape(64), col_new)


def solution(mesh):
    placed = (P(("row", "col"), None), P(("row", "col"), None), P("row"), P(None, "col"))
    return jax.shard_map(
        on_device,
        mesh=mesh,
        in_specs=placed,
        out_specs=(P("row", "col"), P("row"), P(None, "col")),
        check_vma=False,
    )
```

```python
import functools
import jax
import jax.numpy as jnp
from jax import lax
from jax.experimental import pallas as pl
from jax.experimental.pallas import tpu as pltpu
from jax.sharding import PartitionSpec as P

D = 8192
HEAD_DIM = 256
TOKENS = 131072
DECAY_RATE = 1.0 - 8.0 ** (-0.8)
EPSILON = 1e-30
CLIP_LIMIT = 1.0
MIB = 1024 * 1024
SMALL = pltpu.CompilerParams(vmem_limit_bytes=4 * MIB)
GRANTS = (52, 44, 20, 20)

RING4 = ((1, 3), (3, 1))
RING8 = (1, 2, 6, 4)
Z_MASKS = [i * RING8[0] ^ j * RING8[1] ^ k * RING8[2] for i in (0, 1) for j in (0, 1) for k in (0, 1)]
UNITS = ((0, 6), (6, 11), (11, 16))


def swap_cores(value):
    return lax.ppermute(value, "col", [(i, i ^ 1) for i in range(32)])


def along(axis, step, value):
    if axis == "z":
        pairs = []
        for z in range(8):
            for i in range(32):
                core = i % 2
                to = ((((z + core) % 8) ^ RING8[step]) + 8 - core) % 8
                pairs.append((z * 32 + i, to * 32 + i))
        return lax.ppermute(value, ("row", "col"), pairs)
    unit = sum({"x": 8, "y": 2}[name] for name in axis)
    return lax.ppermute(value, "col", [(i, i ^ (RING4[i % 2][step] * unit)) for i in range(32)])


def partial_kernel(chunk, to_sibling, pos, *refs):
    bit = 1 - pl.program_id(0)
    z, core = pos[0], lax.rem(pos[1], 2)
    core = 1 - core if to_sibling else core
    xs, y = refs[:4], refs[4]
    if to_sibling:
        full = refs[5]
    else:
        got, a, b_send, b_keep, c = refs[5:]
    slots = []
    for place in range(8):
        mask = lax.rem(place + core, 8) ^ lax.rem(z + core, 8)
        high = lax.div(mask, 4)
        slots.append(lax.rem(mask, 2) * 4 + (lax.rem(lax.div(mask, 2), 2) ^ high) * 2 + high)
    for s in range(4):
        value = lax.dot_general(
            xs[s][...], y[...], (((0,), (0,)), ((), ())), preferred_element_type=jnp.float32
        )
        for place, slot in enumerate(slots):
            for unit in range(16):
                group, lane = divmod(unit, 4)
                top = place * 32 + group * 8
                piece = value[top : top + 8, lane * 128 : lane * 128 + 128]
                if to_sibling:
                    full[bit, s, slot, unit] = piece
                    continue
                piece = piece + got[bit, s, slot, unit]
                if unit < UNITS[0][1]:
                    a[bit, s, slot, unit] = piece
                elif unit < UNITS[1][1]:
                    (b_send if s >= 2 else b_keep)[bit, s % 2, slot, unit - UNITS[1][0]] = piece
                else:
                    c[bit, s, slot, unit - UNITS[2][0]] = piece


def partial(pos, x, y, chunk, grant, got=None):
    to_sibling = got is None
    na, nb, nc = (to - start for start, to in UNITS)

    def block(s):
        def index(step, pos):
            core = lax.rem(pos[1], 2)
            core = 1 - core if to_sibling else core
            first, second = 1 + 2 * core, 3 - 2 * core
            xi = lax.div(pos[1], 8) ^ (first * (1 - step)) ^ (second * chunk)
            yi = lax.rem(lax.div(pos[1], 2), 4) ^ (first * (s // 2)) ^ (second * (s % 2))
            return (0, (xi * 4 + yi) * 2 + core)

        return pl.BlockSpec((512, 256), index)

    if to_sibling:
        shapes = [(2, 4, 8, 16, 8, 128)]
    else:
        part_b, part_c = (2, 2, 8, nb, 8, 128), (2, 4, 8, nc, 8, 128)
        shapes = [(2, 4, 8, na, 8, 128), part_b, part_b, part_c]
    whole = pl.BlockSpec(memory_space=pltpu.VMEM)
    return pl.pallas_call(
        functools.partial(partial_kernel, chunk, to_sibling),
        grid_spec=pltpu.PrefetchScalarGridSpec(
            num_scalar_prefetch=1,
            grid=(2,),
            in_specs=[block(s) for s in range(4)]
            + [pl.BlockSpec((512, 512), lambda step, pos: (0, 0))]
            + ([] if to_sibling else [whole]),
            out_specs=[whole] * len(shapes),
        ),
        out_shape=[pltpu.VMEM(s, jnp.float32) for s in shapes],
        compiler_params=pltpu.CompilerParams(vmem_limit_bytes=grant * MIB),
        cost_estimate=pl.CostEstimate(
            flops=2 * 512 * 512 * 2048, bytes_accessed=(7 if to_sibling else 11) * MIB, transcendentals=0
        ),
        name=("away" if to_sibling else "near") + str(chunk),
    )(pos, x, x, x, x, y, *([] if to_sibling else [got]))


def stats_kernel(pos, units, col_old, row_old, tile, stats):
    z = pos[0]
    lane = lax.broadcasted_iota(jnp.int32, (8, 128), 1)
    sub = lax.broadcasted_iota(jnp.int32, (8, 128), 0)
    even = lane % 2 == 0
    upper = lane >= 64
    scale = float(TOKENS) ** -0.5
    place = 64 + 32 * lax.rem(z, 2)
    col_row = [jnp.zeros((1, 128), jnp.float32)] * 2
    squares_of = [jnp.zeros((1, 128), jnp.float32)] * 4
    raised_of = [jnp.zeros((1, 128), jnp.float32)] * 4
    for group in range(4):
        grads = [units[group * 4 + i] * scale for i in range(4)]
        square = [g * g for g in grads]
        total = sum(s + EPSILON for s in square)
        sums = [
            jnp.sum(jnp.where(even, total, 0.0), axis=1, keepdims=True),
            jnp.sum(jnp.where(even, 0.0, total), axis=1, keepdims=True),
        ]
        factor = []
        for m in range(2):
            old = col_old[group * 8 : group * 8 + 8, m : m + 1]
            new = DECAY_RATE * old + (1.0 - DECAY_RATE) * (sums[m] / HEAD_DIM)
            new = jnp.broadcast_to(new, (8, 128))
            factor.append(new)
            placed = jnp.where(lane == sub + (group * 8 + place), new, 0.0)
            col_row[m] = col_row[m] + jnp.sum(placed, axis=0, keepdims=True)
        inverse = lax.rsqrt(jnp.where(even, factor[0], factor[1]))
        for i in range(4):
            scaled = grads[i] * inverse
            squares_of[i] = squares_of[i] + jnp.sum(square[i] + EPSILON, axis=0, keepdims=True)
            raised_of[i] = raised_of[i] + jnp.sum(scaled * scaled, axis=0, keepdims=True)
            low = jnp.where(upper, 0.0, scaled)
            high = jnp.where(upper, 0.0, pltpu.roll(scaled, 64, 1))
            tile[2 * i, group * 8 : group * 8 + 8] = low
            tile[2 * i + 1, group * 8 : group * 8 + 8] = high
    value = jnp.zeros((8, 128), jnp.float32)
    for i, row in enumerate(squares_of + raised_of):
        value = jnp.where(sub == i, jnp.broadcast_to(row, (8, 128)), value)
    for to in range(32):
        stats[to] = value
    olds = jnp.where((sub == z) & upper, jnp.broadcast_to(row_old[...], (8, 128)), 0.0)
    cols = jnp.zeros((8, 128), jnp.float32)
    for m in range(2):
        cols = jnp.where(sub == 4 * m + lax.div(z, 2), jnp.broadcast_to(col_row[m], (8, 128)), cols)
    for to in range(8):
        tile[to, 16:24] = tile[to, 16:24] + olds
        tile[to, 24:32] = tile[to, 24:32] + cols


def pack_kernel(tile, stats, load):
    sub = lax.broadcasted_iota(jnp.int32, (8, 128), 0)
    upper = lax.broadcasted_iota(jnp.int32, (8, 128), 1) >= 64
    sums = [stats[i] for i in range(32)]
    while len(sums) > 1:
        sums = [p + q for p, q in zip(sums[::2], sums[1::2])]
    placed = []
    for base in (0, 4):
        value = jnp.zeros((8, 128), jnp.float32)
        for i in range(4):
            both = jnp.broadcast_to(sums[0][base + i : base + i + 1], (8, 128))
            value = jnp.where(sub == 2 * i, pltpu.roll(both, 64, 1), value)
            value = jnp.where(sub == 2 * i + 1, both, value)
        placed.append(jnp.where(upper, value, 0.0))
    for to in range(8):
        load[to, 0:8] = tile[to, 0:8] + placed[0]
        load[to, 8:16] = tile[to, 8:16] + placed[1]
        load[to, 16:32] = tile[to, 16:32]


def finish_kernel(pos, load, direction, row_new, col_new, scales, rows):
    z = pos[0]
    lane = lax.broadcasted_iota(jnp.int32, (8, 128), 1)
    even = lane % 2 == 0
    upper = lane >= 64
    total = load[0]
    for i in range(1, 8):
        total = total + load[i]
    row_all = DECAY_RATE * total[16:24] + (1.0 - DECAY_RATE) * (total[0:8] / D)
    row_all = jnp.where(upper, row_all, 1.0)
    per_row = jnp.where(upper, total[8:16] / row_all, 0.0)
    limiter = []
    for keep in (even, jnp.logical_not(even)):
        clip = jnp.sum(jnp.where(keep, per_row, 0.0), axis=(0, 1), keepdims=True)
        limiter.append(jnp.maximum(1.0, jnp.sqrt(clip / (HEAD_DIM * D)) / CLIP_LIMIT))
    bound = jnp.where(even, jnp.broadcast_to(limiter[0], (8, 128)), jnp.broadcast_to(limiter[1], (8, 128)))
    scales[...] = pltpu.roll(lax.rsqrt(row_all) / bound, 64, 1)
    rows[...] = pltpu.roll(row_all, 64, 1)
    row_new[...] = rows[pl.ds(z, 1), 0:64]
    mine = jnp.broadcast_to(scales[pl.ds(z, 1), :], (128, 128))
    for half in range(2):
        block = jnp.concatenate([load[4 * half + i] for i in range(4)], axis=0) * mine
        direction[:, half * 128 : half * 128 + 128] = block.T[0:64]
    cols = total[24:32]
    moved = pltpu.roll(cols, 64, 1)
    for m in range(2):
        for half in range(2):
            at = 4 * m + 2 * half
            pair = jnp.where(upper[0:1], cols[at + 1 : at + 2], moved[at : at + 1])
            col_new[m : m + 1, half * 128 : half * 128 + 128] = pair


def on_device(activations, kv_grads, row_state, col_state):
    z = lax.axis_index("row").astype(jnp.int32)
    pos = jnp.stack([z, lax.axis_index("col").astype(jnp.int32)])
    col_old = lax.dynamic_slice_in_dim(col_state, z * 32, 32, axis=1).T
    row_old = jnp.concatenate([row_state, row_state]).reshape(1, 128)

    x, y = activations, kv_grads
    na, nb, nc = (to - start for start, to in UNITS)
    sent = [swap_cores(partial(pos, x, y, 1 - i, GRANTS[i])[0]) for i in (0, 1)]
    streams = [None, None]
    for i in (0, 1):
        a, b_send, b_keep, c = partial(pos, x, y, 1 - i, GRANTS[2 + i], sent[i])
        a = a.reshape(2, 2, 2, 2, 2, 2, na, 8, 128)
        b_send, b_keep = (v.reshape(2, 2, 2, 2, 2, nb, 8, 128) for v in (b_send, b_keep))
        c = c.reshape(2, 2, 2, 2, 2, 2, nc, 8, 128)

        got = along("x", 0, a[1]), along("y", 0, b_send), along("z", 0, c[:, :, :, 1])
        a, b, c = a[0], b_keep, c[:, :, :, 0]
        ga, gb, gc = lax.optimization_barrier(got)

        a_send, b_send, c_send = a[1] + ga[1], b[:, :, 1] + gb[:, :, 1], c[1] + gc[1]
        got = along("y", 0, a_send), along("z", 0, b_send), along("x", 0, c_send)
        a, b, c = a[0] + ga[0], b[:, :, 0] + gb[:, :, 0], c[0] + gc[0]
        ga, gb, gc = lax.optimization_barrier(got)

        a_send, b_send, c_send = a[:, 1] + ga[:, 1], b[1] + gb[1], c[1] + gc[1]
        got = along("z", 0, a_send), along("x", 0, b_send), along("y", 0, c_send)
        a, b, c = a[:, 0] + ga[:, 0], b[0] + gb[0], c[0] + gc[0]
        ga, gb, gc = lax.optimization_barrier(got)
        streams[1 - i] = ((a, ga), (b, gb), (c, gc))

    def quarter(i, j):
        return jnp.concatenate([v[j] + g[j] for v, g in streams[i]], axis=2)

    got = along("xy", 1, quarter(1, 1)), along("x", 1, quarter(1, 0)), along("y", 1, quarter(0, 1))
    value = quarter(0, 0) + got[0] + got[1] + got[2]
    got = along("z", 3, value[1, 1]), along("z", 1, value[1, 0]), along("z", 2, value[0, 1])
    value = value[0, 0] + got[0] + got[1] + got[2]

    tile, stats = pl.pallas_call(
        stats_kernel,
        in_specs=[pl.BlockSpec(memory_space=pltpu.SMEM)] + [pl.BlockSpec(memory_space=pltpu.VMEM)] * 3,
        out_specs=[pl.BlockSpec(memory_space=pltpu.VMEM)] * 2,
        out_shape=[
            pltpu.VMEM((8, 32, 128), jnp.float32),
            pltpu.VMEM((32, 8, 128), jnp.float32),
        ],
        compiler_params=SMALL,
        name="stats",
    )(pos, value, col_old, row_old)

    stats = lax.all_to_all(stats, "col", 0, 0, tiled=True)
    load = pl.pallas_call(
        pack_kernel,
        in_specs=[pl.BlockSpec(memory_space=pltpu.VMEM)] * 2,
        out_specs=pl.BlockSpec(memory_space=pltpu.VMEM),
        out_shape=pltpu.VMEM((8, 32, 128), jnp.float32),
        compiler_params=SMALL,
        name="pack",
    )(tile, stats)
    load = lax.all_to_all(load, "row", 0, 0, tiled=True)

    direction, row_new, col_new = pl.pallas_call(
        finish_kernel,
        in_specs=[pl.BlockSpec(memory_space=pltpu.SMEM), pl.BlockSpec(memory_space=pltpu.VMEM)],
        out_specs=[pl.BlockSpec(memory_space=pltpu.VMEM)] * 3,
        out_shape=[
            jax.ShapeDtypeStruct((64, 256), jnp.float32),
            jax.ShapeDtypeStruct((1, 64), jnp.float32),
            jax.ShapeDtypeStruct((2, 256), jnp.float32),
        ],
        scratch_shapes=[pltpu.VMEM((8, 128), jnp.float32)] * 2,
        compiler_params=SMALL,
        name="finish",
    )(pos, load)
    return (direction, row_new.reshape(64), col_new)


def solution(mesh):
    placed = (P(("row", "col"), None), P(("row", "col"), None), P("row"), P(None, "col"))
    return jax.shard_map(
        on_device,
        mesh=mesh,
        in_specs=placed,
        out_specs=(P("row", "col"), P("row"), P(None, "col")),
        check_vma=False,
    )
```

```python
import functools
import jax
import jax.numpy as jnp
from jax import lax
from jax.experimental import pallas as pl
from jax.experimental.pallas import tpu as pltpu
from jax.sharding import PartitionSpec as P

D = 8192
HEAD_DIM = 256
TOKENS = 131072
DECAY_RATE = 1.0 - 8.0 ** (-0.8)
EPSILON = 1e-30
CLIP_LIMIT = 1.0
MIB = 1024 * 1024
SMALL = pltpu.CompilerParams(vmem_limit_bytes=4 * MIB)
GRANTS = (52, 44, 20, 20)

RING4 = ((1, 3), (3, 1))
RING8 = (1, 2, 7, 5)
Z_MASKS = [i * RING8[0] ^ j * RING8[1] ^ k * RING8[2] for i in (0, 1) for j in (0, 1) for k in (0, 1)]
UNITS = ((0, 6), (6, 11), (11, 16))


def swap_cores(value):
    return lax.ppermute(value, "col", [(i, i ^ 1) for i in range(32)])


def along(axis, step, value):
    if axis == "z":
        pairs = []
        for z in range(8):
            for i in range(32):
                core = i % 2
                to = ((((z + core) % 8) ^ RING8[step]) + 8 - core) % 8
                pairs.append((z * 32 + i, to * 32 + i))
        return lax.ppermute(value, ("row", "col"), pairs)
    unit = sum({"x": 8, "y": 2}[name] for name in axis)
    return lax.ppermute(value, "col", [(i, i ^ (RING4[i % 2][step] * unit)) for i in range(32)])


def partial_kernel(chunk, to_sibling, *refs):
    bit = 1 - pl.program_id(0)
    z, core = lax.axis_index("row"), lax.rem(lax.axis_index("col"), 2)
    core = 1 - core if to_sibling else core
    xs, y = refs[:4], refs[4]
    if to_sibling:
        full = refs[5]
    else:
        got, a, b_send, b_keep, c = refs[5:]
    slots = []
    for place in range(8):
        mask = lax.rem(place + core, 8) ^ lax.rem(z + core, 8)
        high = lax.div(mask, 4)
        slots.append((lax.rem(mask, 2) ^ high) * 4 + (lax.rem(lax.div(mask, 2), 2) ^ high) * 2 + high)
    for s in range(4):
        value = lax.dot_general(
            xs[s][...], y[...], (((0,), (0,)), ((), ())), preferred_element_type=jnp.float32
        )
        for place, slot in enumerate(slots):
            for unit in range(16):
                group, lane = divmod(unit, 4)
                top = place * 32 + group * 8
                piece = value[top : top + 8, lane * 128 : lane * 128 + 128]
                if to_sibling:
                    full[bit, s, slot, unit] = piece
                    continue
                piece = piece + got[bit, s, slot, unit]
                if unit < UNITS[0][1]:
                    a[bit, s, slot, unit] = piece
                elif unit < UNITS[1][1]:
                    (b_send if s >= 2 else b_keep)[bit, s % 2, slot, unit - UNITS[1][0]] = piece
                else:
                    c[bit, s, slot, unit - UNITS[2][0]] = piece


def partial(x, y, chunk, grant, got=None):
    to_sibling = got is None
    na, nb, nc = (to - start for start, to in UNITS)

    def block(s):
        def index(step):
            col = lax.axis_index("col")
            core = lax.rem(col, 2)
            core = 1 - core if to_sibling else core
            first, second = 1 + 2 * core, 3 - 2 * core
            xi = lax.div(col, 8) ^ (first * (1 - step)) ^ (second * chunk)
            yi = lax.rem(lax.div(col, 2), 4) ^ (first * (s // 2)) ^ (second * (s % 2))
            return (0, (xi * 4 + yi) * 2 + core)

        return pl.BlockSpec((512, 256), index)

    if to_sibling:
        shapes = [(2, 4, 8, 16, 8, 128)]
    else:
        part_b, part_c = (2, 2, 8, nb, 8, 128), (2, 4, 8, nc, 8, 128)
        shapes = [(2, 4, 8, na, 8, 128), part_b, part_b, part_c]
    whole = pl.BlockSpec(memory_space=pltpu.VMEM)
    return pl.pallas_call(
        functools.partial(partial_kernel, chunk, to_sibling),
        grid=(2,),
        in_specs=[block(s) for s in range(4)]
        + [pl.BlockSpec((512, 512), lambda step: (0, 0))]
        + ([] if to_sibling else [whole]),
        out_specs=[whole] * len(shapes),
        out_shape=[pltpu.VMEM(s, jnp.float32) for s in shapes],
        compiler_params=pltpu.CompilerParams(vmem_limit_bytes=grant * MIB),
        cost_estimate=pl.CostEstimate(
            flops=2 * 512 * 512 * 2048, bytes_accessed=(7 if to_sibling else 11) * MIB, transcendentals=0
        ),
        name=("away" if to_sibling else "near") + str(chunk),
    )(x, x, x, x, y, *([] if to_sibling else [got]))


def stats_kernel(units, col_old, row_old, tile, stats):
    z = lax.axis_index("row")
    lane = lax.broadcasted_iota(jnp.int32, (8, 128), 1)
    sub = lax.broadcasted_iota(jnp.int32, (8, 128), 0)
    even = lane % 2 == 0
    upper = lane >= 64
    scale = float(TOKENS) ** -0.5
    place = 64 + 32 * lax.rem(z, 2)
    col_row = [jnp.zeros((1, 128), jnp.float32)] * 2
    squares_of = [jnp.zeros((1, 128), jnp.float32)] * 4
    raised_of = [jnp.zeros((1, 128), jnp.float32)] * 4
    for group in range(4):
        grads = [units[group * 4 + i] * scale for i in range(4)]
        square = [g * g for g in grads]
        total = sum(s + EPSILON for s in square)
        sums = [
            jnp.sum(jnp.where(even, total, 0.0), axis=1, keepdims=True),
            jnp.sum(jnp.where(even, 0.0, total), axis=1, keepdims=True),
        ]
        factor = []
        for m in range(2):
            old = col_old[group * 8 : group * 8 + 8, m : m + 1]
            new = DECAY_RATE * old + (1.0 - DECAY_RATE) * (sums[m] / HEAD_DIM)
            new = jnp.broadcast_to(new, (8, 128))
            factor.append(new)
            placed = jnp.where(lane == sub + (group * 8 + place), new, 0.0)
            col_row[m] = col_row[m] + jnp.sum(placed, axis=0, keepdims=True)
        inverse = lax.rsqrt(jnp.where(even, factor[0], factor[1]))
        for i in range(4):
            scaled = grads[i] * inverse
            squares_of[i] = squares_of[i] + jnp.sum(square[i] + EPSILON, axis=0, keepdims=True)
            raised_of[i] = raised_of[i] + jnp.sum(scaled * scaled, axis=0, keepdims=True)
            low = jnp.where(upper, 0.0, scaled)
            high = jnp.where(upper, 0.0, pltpu.roll(scaled, 64, 1))
            tile[2 * i, group * 8 : group * 8 + 8] = low
            tile[2 * i + 1, group * 8 : group * 8 + 8] = high
    value = jnp.zeros((8, 128), jnp.float32)
    for i, row in enumerate(squares_of + raised_of):
        value = jnp.where(sub == i, jnp.broadcast_to(row, (8, 128)), value)
    for to in range(32):
        stats[to] = value
    olds = jnp.where((sub == z) & upper, jnp.broadcast_to(row_old[...], (8, 128)), 0.0)
    cols = jnp.zeros((8, 128), jnp.float32)
    for m in range(2):
        cols = jnp.where(sub == 4 * m + lax.div(z, 2), jnp.broadcast_to(col_row[m], (8, 128)), cols)
    for to in range(8):
        tile[to, 16:24] = tile[to, 16:24] + olds
        tile[to, 24:32] = tile[to, 24:32] + cols


def pack_kernel(tile, stats, load):
    sub = lax.broadcasted_iota(jnp.int32, (8, 128), 0)
    upper = lax.broadcasted_iota(jnp.int32, (8, 128), 1) >= 64
    sums = [stats[i] for i in range(32)]
    while len(sums) > 1:
        sums = [p + q for p, q in zip(sums[::2], sums[1::2])]
    placed = []
    for base in (0, 4):
        value = jnp.zeros((8, 128), jnp.float32)
        for i in range(4):
            both = jnp.broadcast_to(sums[0][base + i : base + i + 1], (8, 128))
            value = jnp.where(sub == 2 * i, pltpu.roll(both, 64, 1), value)
            value = jnp.where(sub == 2 * i + 1, both, value)
        placed.append(jnp.where(upper, value, 0.0))
    for to in range(8):
        load[to, 0:8] = tile[to, 0:8] + placed[0]
        load[to, 8:16] = tile[to, 8:16] + placed[1]
        load[to, 16:32] = tile[to, 16:32]


def finish_kernel(load, direction, row_new, col_new, scales, rows):
    z = lax.axis_index("row")
    lane = lax.broadcasted_iota(jnp.int32, (8, 128), 1)
    even = lane % 2 == 0
    upper = lane >= 64
    total = load[0]
    for i in range(1, 8):
        total = total + load[i]
    row_all = DECAY_RATE * total[16:24] + (1.0 - DECAY_RATE) * (total[0:8] / D)
    row_all = jnp.where(upper, row_all, 1.0)
    per_row = jnp.where(upper, total[8:16] / row_all, 0.0)
    limiter = []
    for keep in (even, jnp.logical_not(even)):
        clip = jnp.sum(jnp.where(keep, per_row, 0.0), axis=(0, 1), keepdims=True)
        limiter.append(jnp.maximum(1.0, jnp.sqrt(clip / (HEAD_DIM * D)) / CLIP_LIMIT))
    bound = jnp.where(even, jnp.broadcast_to(limiter[0], (8, 128)), jnp.broadcast_to(limiter[1], (8, 128)))
    scales[...] = pltpu.roll(lax.rsqrt(row_all) / bound, 64, 1)
    rows[...] = pltpu.roll(row_all, 64, 1)
    row_new[...] = rows[pl.ds(z, 1), 0:64]
    mine = jnp.broadcast_to(scales[pl.ds(z, 1), :], (128, 128))
    for half in range(2):
        block = jnp.concatenate([load[4 * half + i] for i in range(4)], axis=0) * mine
        direction[:, half * 128 : half * 128 + 128] = block.T[0:64]
    cols = total[24:32]
    moved = pltpu.roll(cols, 64, 1)
    for m in range(2):
        for half in range(2):
            at = 4 * m + 2 * half
            pair = jnp.where(upper[0:1], cols[at + 1 : at + 2], moved[at : at + 1])
            col_new[m : m + 1, half * 128 : half * 128 + 128] = pair


def on_device(activations, kv_grads, row_state, col_state):
    z = lax.axis_index("row").astype(jnp.int32)
    col_old = lax.dynamic_slice_in_dim(col_state, z * 32, 32, axis=1).T
    row_old = jnp.concatenate([row_state, row_state]).reshape(1, 128)

    x, y = activations, kv_grads
    na, nb, nc = (to - start for start, to in UNITS)
    sent = [swap_cores(partial(x, y, 1 - i, GRANTS[i])[0]) for i in (0, 1)]
    streams = [None, None]
    for i in (0, 1):
        a, b_send, b_keep, c = partial(x, y, 1 - i, GRANTS[2 + i], sent[i])
        a = a.reshape(2, 2, 2, 2, 2, 2, na, 8, 128)
        b_send, b_keep = (v.reshape(2, 2, 2, 2, 2, nb, 8, 128) for v in (b_send, b_keep))
        c = c.reshape(2, 2, 2, 2, 2, 2, nc, 8, 128)

        got = along("x", 0, a[1]), along("y", 0, b_send), along("z", 0, c[:, :, :, 1])
        a, b, c = a[0], b_keep, c[:, :, :, 0]
        ga, gb, gc = lax.optimization_barrier(got)

        a_send, b_send, c_send = a[1] + ga[1], b[:, :, 1] + gb[:, :, 1], c[1] + gc[1]
        got = along("y", 0, a_send), along("z", 0, b_send), along("x", 0, c_send)
        a, b, c = a[0] + ga[0], b[:, :, 0] + gb[:, :, 0], c[0] + gc[0]
        ga, gb, gc = lax.optimization_barrier(got)

        a_send, b_send, c_send = a[:, 1] + ga[:, 1], b[1] + gb[1], c[1] + gc[1]
        got = along("z", 0, a_send), along("x", 0, b_send), along("y", 0, c_send)
        a, b, c = a[:, 0] + ga[:, 0], b[0] + gb[0], c[0] + gc[0]
        ga, gb, gc = lax.optimization_barrier(got)
        streams[1 - i] = ((a, ga), (b, gb), (c, gc))

    def quarter(i, j):
        return jnp.concatenate([v[j] + g[j] for v, g in streams[i]], axis=2)

    got = along("xy", 1, quarter(1, 1)), along("x", 1, quarter(1, 0)), along("y", 1, quarter(0, 1))
    value = quarter(0, 0) + got[0] + got[1] + got[2]
    got = along("z", 3, value[1, 1]), along("z", 1, value[1, 0]), along("z", 2, value[0, 1])
    value = value[0, 0] + got[0] + got[1] + got[2]

    tile, stats = pl.pallas_call(
        stats_kernel,
        in_specs=[pl.BlockSpec(memory_space=pltpu.VMEM)] * 3,
        out_specs=[pl.BlockSpec(memory_space=pltpu.VMEM)] * 2,
        out_shape=[
            pltpu.VMEM((8, 32, 128), jnp.float32),
            pltpu.VMEM((32, 8, 128), jnp.float32),
        ],
        compiler_params=SMALL,
        name="stats",
    )(value, col_old, row_old)

    stats = lax.all_to_all(stats, "col", 0, 0, tiled=True)
    load = pl.pallas_call(
        pack_kernel,
        in_specs=[pl.BlockSpec(memory_space=pltpu.VMEM)] * 2,
        out_specs=pl.BlockSpec(memory_space=pltpu.VMEM),
        out_shape=pltpu.VMEM((8, 32, 128), jnp.float32),
        compiler_params=SMALL,
        name="pack",
    )(tile, stats)
    load = lax.all_to_all(load, "row", 0, 0, tiled=True)

    direction, row_new, col_new = pl.pallas_call(
        finish_kernel,
        in_specs=[pl.BlockSpec(memory_space=pltpu.VMEM)],
        out_specs=[pl.BlockSpec(memory_space=pltpu.VMEM)] * 3,
        out_shape=[
            jax.ShapeDtypeStruct((64, 256), jnp.float32),
            jax.ShapeDtypeStruct((1, 64), jnp.float32),
            jax.ShapeDtypeStruct((2, 256), jnp.float32),
        ],
        scratch_shapes=[pltpu.VMEM((8, 128), jnp.float32)] * 2,
        compiler_params=SMALL,
        name="finish",
    )(load)
    return (direction, row_new.reshape(64), col_new)


def solution(mesh):
    placed = (P(("row", "col"), None), P(("row", "col"), None), P("row"), P(None, "col"))
    return jax.shard_map(
        on_device,
        mesh=mesh,
        in_specs=placed,
        out_specs=(P("row", "col"), P("row"), P(None, "col")),
        check_vma=False,
    )
```
